32 devices in a mesh: depth: 16 (over z, y, x), rays: 2 (over core).
Axes of the slice: x: 2, y: 2, z: 4, core: 2. Of those that a mesh axis runs over, the one named last changes fastest.
Arguments:
- encoded: bfloat16 [16, 4, 1024, 256], P('depth', None, 'rays'), may hold values from -6 to 6
- deltas: float32 [16, 4, 1024], P('depth', None, 'rays'), may hold values from 0.015625 to 0.125
- w_in: bfloat16 [16, 256, 512], P('depth'), may hold values from -0.375 to 0.375
- w_mid: bfloat16 [16, 512, 512], P('depth'), may hold values from -0.25 to 0.25
- w_sigma: bfloat16 [16, 512], P('depth'), may hold values from -0.25 to 0.25
- order: int32 [2, 16], P('rays'), may hold values from 0 to 15, each once within a row
- target: bfloat16 [1024, 512], P('rays'), may hold values from -3 to 3
Outputs:
- grad_in: float32 [16, 256, 512], P('depth', 'rays')
- grad_mid: float32 [16, 512, 512], P('depth', 'rays')
- grad_sigma: float32 [16, 512], P('depth', 'rays')
- loss: float32 [], replicated
The draws below stay inside these ranges and needn't reach their ends.
Inputs may be any that keep to these rules, and one draw needn't show every extreme that they name: Each row of order lists every region once.
All inputs are finite; a program needn't handle non-finite values.
Results may differ from the reference program's by a relative error of at most 0.015.
Values may be sent and summed in bfloat16 or wider, within the bound.
No kernel may reach another device: no remote copies, remote signals or barrier semaphores. Data moves between devices by JAX's collectives and lax.ppermute only.
A program may use at most 64 MiB of HBM per device.

```python
import math
import jax
import jax.numpy as jnp
from jax import lax

E = 256
H = 512
F = 512
S = 4
R_DEV = 512
REGIONS = 16
GROUPS = 2
RAYS = 1024


def strengthened(values, stream_key, source, target, shards_of, factor):
    def block_of(dim):
        return (jnp.arange(values.shape[dim]) // (values.shape[dim] // shards_of)).reshape((-1,) + (1,) * (values.ndim - 1 - dim))

    near = jax.random.permutation(stream_key, shards_of)[block_of(target)]
    far = (block_of(target) + shards_of // 2) % shards_of
    return jnp.where((block_of(source) == near) | (block_of(source) == far), factor * values, values)


def level_of(key, shape, split, low, high):
    gain, own = 1.0, jax.random.fold_in(key, 6)
    for axis_at, parts in split:
        heights = jnp.exp(jax.random.uniform(jax.random.fold_in(own, axis_at), (parts,), jnp.float32, low / len(split), high / len(split)))
        gain = gain * jnp.repeat(heights, shape[axis_at] // parts).reshape([-1 if axis == axis_at else 1 for axis in range(len(shape))])
    return gain


def noise(stream_key, shape, width, most, split=(), kind=jnp.bfloat16):
    loudness = level_of(stream_key, shape, split, -0.22, 0.18) if split else 1.0
    array = jax.random.normal(stream_key, shape, jnp.float32) * width * loudness
    return jnp.minimum(jnp.maximum(array, -most), most).astype(kind)


def noise_with(own_key, dims, width, bound, cuts, heavy, kind=jnp.bfloat16):
    values = width * jax.random.normal(own_key, dims, jnp.float32)
    if cuts:
        values = values * level_of(own_key, dims, cuts, -0.22, 0.18)
    return jnp.clip(strengthened(values, jax.random.fold_in(own_key, 3), *heavy), -bound, bound).astype(kind)


def setup_inputs(seed: int = 0) -> dict:
    keys = jax.random.split(jax.random.key(seed), 8)
    return {
        "encoded": noise_with(keys[0], (REGIONS, S, RAYS, E), 1.0, 6.0, ((0, 16), (2, 2)), (2, 3, 2, 2.0)),
        "deltas": jnp.clip(jnp.exp(math.log(0.125) - 2.0794415 * jax.random.uniform(keys[1], (REGIONS, S, RAYS), jnp.float32) ** level_of(keys[1], (REGIONS, S, RAYS), ((0, 16), (2, 2)), -0.2, 0.2)), 0.015625, 0.125),
        "w_in": noise(keys[2], (REGIONS, E, H), E ** -0.5, 0.375, ((0, 16),)),
        "w_mid": noise(keys[3], (REGIONS, H, F), H ** -0.5, 0.25, ((0, 16),)),
        "w_sigma": noise(keys[4], (REGIONS, H), H ** -0.5, 0.25, ((0, 16),)),
        "order": jax.vmap(lambda own: jax.random.permutation(own, REGIONS))(jax.random.split(keys[5], GROUPS)).reshape((GROUPS, REGIONS)).astype(jnp.int32),
        "target": noise(keys[6], (RAYS, F), 0.5, 3.0, ((0, 2),)),
    }


def local_fields(x, w1, w2, ws, delta):
    rows = x.reshape(-1, x.shape[-1])
    hidden = jnp.maximum(jnp.dot(rows, w1, preferred_element_type=jnp.float32), 0.0)
    hidden_b = hidden.astype(jnp.bfloat16)
    feat = jnp.dot(hidden_b, w2, preferred_element_type=jnp.float32)
    logit = jnp.dot(hidden_b, ws, preferred_element_type=jnp.float32)
    tau = jax.nn.softplus(logit).reshape(delta.shape) * delta
    excl = jnp.cumsum(tau, axis=0) - tau
    weight = jnp.exp(-excl) * (1.0 - jnp.exp(-tau))
    return rows, hidden, hidden_b, feat, logit, tau, excl, weight


def region_forward(args):
    x, w1, w2, ws, delta = args
    rows, hidden, hidden_b, feat, logit, tau, excl, weight = local_fields(x, w1, w2, ws, delta)
    feat3 = feat.reshape(S, -1, F)
    segment = jnp.sum(weight[:, :, None] * feat3, axis=0)
    return segment, jnp.sum(tau, axis=0)


def region_backward(args, dcolor):
    x, w1, w2, ws, delta, trans, gtau = args
    rows, hidden, hidden_b, feat, logit, tau, excl, weight = local_fields(x, w1, w2, ws, delta)
    dseg = trans[:, None] * dcolor
    feat3 = feat.reshape(S, -1, F)
    dfeat = (weight[:, :, None] * dseg[None]).astype(jnp.bfloat16)
    vsum = jnp.sum(feat3 * dseg[None], axis=2)
    wv = weight * vsum
    dtau = jnp.exp(-(excl + tau)) * vsum - (jnp.sum(wv, axis=0)[None] - jnp.cumsum(wv, axis=0)) + gtau[None]
    dz = (dtau * delta).reshape(-1) * jax.nn.sigmoid(logit)
    dfeat2 = dfeat.reshape(-1, F)
    dhb = jnp.dot(dfeat2, w2.T, preferred_element_type=jnp.float32) + dz[:, None] * ws.astype(jnp.float32)[None]
    dpre = jnp.where(hidden > 0, dhb, 0.0).astype(jnp.bfloat16)
    x4 = rows.reshape(S, GROUPS, R_DEV, E).astype(jnp.float32)
    p4 = dpre.reshape(S, GROUPS, R_DEV, H).astype(jnp.float32)
    h4 = hidden_b.reshape(S, GROUPS, R_DEV, H).astype(jnp.float32)
    f4 = dfeat2.reshape(S, GROUPS, R_DEV, F).astype(jnp.float32)
    z4 = dz.reshape(S, GROUPS, R_DEV)
    part_in = jnp.einsum('sgre,sgrh->geh', x4, p4, precision=lax.Precision.HIGHEST)
    part_mid = jnp.einsum('sgrh,sgrf->ghf', h4, f4, precision=lax.Precision.HIGHEST)
    part_sig = jnp.einsum('sgrh,sgr->gh', h4, z4, precision=lax.Precision.HIGHEST)

    def settle(part):
        return jnp.sum(lax.optimization_barrier(part.astype(jnp.bfloat16)).astype(jnp.float32), axis=0)

    return settle(part_in), settle(part_mid), settle(part_sig)


def reference(encoded, deltas, w_in, w_mid, w_sigma, order, target):
    segment, depth_tau = lax.map(region_forward, (encoded, w_in, w_mid, w_sigma, deltas))
    positions = jnp.arange(REGIONS, dtype=jnp.int32)
    onehot = order[:, :, None] == positions[None, None, :]
    rank = jnp.sum(jnp.where(onehot, positions[None, :, None], 0), axis=1).astype(jnp.int32)
    before = (rank[:, None, :] < rank[:, :, None]).astype(jnp.float32)
    tau_g = depth_tau.reshape(REGIONS, GROUPS, R_DEV)
    prefix = jnp.einsum('grs,sgi->rgi', before, tau_g, precision=lax.Precision.HIGHEST).reshape(REGIONS, RAYS)
    trans = jnp.exp(-prefix)
    color = jnp.sum(trans[:, :, None] * segment, axis=0)
    err = color - target.astype(jnp.float32)
    loss = jnp.sum(err * err) / (RAYS * F)
    dcolor = lax.optimization_barrier(err.astype(jnp.bfloat16)).astype(jnp.float32)
    qsum = jnp.sum(segment * dcolor[None], axis=2)
    contrib = (trans * qsum).reshape(REGIONS, GROUPS, R_DEV)
    gtau = -jnp.einsum('gsr,sgi->rgi', before, contrib, precision=lax.Precision.HIGHEST).reshape(REGIONS, RAYS)
    grad_in, grad_mid, grad_sigma = lax.map(lambda a: region_backward(a, dcolor), (encoded, w_in, w_mid, w_sigma, deltas, trans, gtau))
    return grad_in, grad_mid, grad_sigma, loss
```

```python
import functools

import jax
import jax.numpy as jnp
from jax import lax
from jax.experimental import pallas as pl
from jax.experimental.pallas import tpu as pltpu
from jax.sharding import PartitionSpec as P

LANES = 128
PAD_ROWS = 16
TAU_ROWS = 8
MIB = 1024 * 1024
F32 = jnp.float32
BF16 = jnp.bfloat16


def split_parts(value):
    first = value.astype(BF16).astype(F32)
    rest = value - first
    second = rest.astype(BF16).astype(F32)
    return first, second, rest - second


def stack_rows(rows, count):
    out = jnp.concatenate(rows, axis=0)
    if out.shape[0] < count:
        out = jnp.concatenate([out, jnp.zeros((count - out.shape[0], LANES), F32)], axis=0)
    return out


def contract(left, right, dims):
    return lax.dot_general(left, right, (dims, ((), ())), preferred_element_type=F32)


def forward_kernel(
    enc_hbm, delta_hbm, w_in_hbm, w_mid_hbm, w_sig_hbm, send_hbm, stat_hbm,
    enc_ref, delta_ref, w_in_ref, w_mid_ref, w_sig_ref, send_ref, hid_ref, stat_ref, sems, out_sems,
):
    samples, rays = enc_ref.shape[:2]
    blocks = rays // LANES
    chunk = rays // send_ref.shape[0]
    width = w_mid_ref.shape[1]
    copies = [
        pltpu.make_async_copy(w_in_hbm.at[0], w_in_ref, sems.at[0]),
        pltpu.make_async_copy(w_sig_hbm, w_sig_ref, sems.at[1]),
        pltpu.make_async_copy(delta_hbm.at[0], delta_ref, sems.at[2]),
        pltpu.make_async_copy(w_mid_hbm.at[0], w_mid_ref, sems.at[3]),
    ]
    enc_copies = [
        pltpu.make_async_copy(enc_hbm.at[0, k], enc_ref.at[k], sems.at[4 + k]) for k in range(samples)
    ]
    leaving = []

    def leave(source, target):
        leaving.append(pltpu.make_async_copy(source, target, out_sems.at[len(leaving)]))
        leaving[-1].start()

    for copy in [copies[0], enc_copies[0], copies[1], *enc_copies[1:], copies[2], copies[3]]:
        copy.start()
    copies[0].wait()
    copies[1].wait()
    w_in = w_in_ref[...]
    w_sig = w_sig_ref[...].astype(F32)
    lanes = lax.broadcasted_iota(jnp.int32, (rays, LANES), 1)
    pack = jnp.zeros((rays, LANES), F32)
    for k in range(samples):
        enc_copies[k].wait()
        hidden = jnp.maximum(contract(enc_ref[k], w_in, ((1,), (0,))), 0.0).astype(BF16)
        hid_ref[k] = hidden
        pack = jnp.where(lanes == k, jnp.sum(hidden.astype(F32) * w_sig, axis=1, keepdims=True), pack)

    copies[2].wait()
    copies[3].wait()
    tall = [slice(b * LANES, (b + 1) * LANES) for b in range(blocks)]
    logit = jnp.concatenate([pack[at].T[:samples] for at in tall], axis=1)
    spacing = delta_ref[...]
    small = jnp.exp(-jnp.abs(logit))
    tau = (jnp.maximum(logit, 0.0) + jnp.log1p(small)) * spacing
    slope = spacing * jnp.where(logit >= 0, 1.0, small) / (1.0 + small)
    fade = jnp.exp(-tau)
    through = jnp.ones((1, rays), F32)
    total = jnp.zeros((1, rays), F32)
    weights, remains = [], []
    for k in range(samples):
        weights.append(through * (1.0 - fade[k : k + 1]))
        through = through * fade[k : k + 1]
        remains.append(through)
        total = total + tau[k : k + 1]
    lines = jnp.concatenate(weights + remains + [slope], axis=0)
    stat = jnp.concatenate([stack_rows([lines[:, at]], LANES).T for at in tall], axis=0)
    stat_ref[:rays] = stat
    mix = stat[:, 0:1] * hid_ref[0].astype(F32)
    for k in range(1, samples):
        mix = mix + stat[:, k : k + 1] * hid_ref[k].astype(F32)
    mix = mix.astype(BF16)
    stat_ref[rays:] = stack_rows([w_sig[:, t * LANES : (t + 1) * LANES] for t in range(w_sig.shape[1] // LANES)], chunk)
    leave(stat_ref, stat_hbm)
    segment = contract(mix, w_mid_ref[...], ((1,), (0,))).astype(BF16)
    for b in range(blocks):
        tau_rows = stack_rows(list(split_parts(total[:, b * LANES : (b + 1) * LANES])), TAU_ROWS)
        for c in range(LANES // chunk):
            to = b * (LANES // chunk) + c
            for t in range(width // LANES):
                send_ref[to, t * chunk : (t + 1) * chunk] = segment[
                    to * chunk : (to + 1) * chunk, t * LANES : (t + 1) * LANES
                ]
            turned = tau_rows if c == 0 else pltpu.roll(tau_rows, LANES - c * chunk, 1)
            send_ref[to, width // LANES * chunk :] = turned.astype(BF16)
        owners = pl.ds(b * (LANES // chunk), LANES // chunk)
        leave(send_ref.at[owners], send_hbm.at[owners])
    for copy in leaving:
        copy.wait()


def composite_kernel(order_ref, me_ref, got_ref, target_ref, reply_ref, tau_ref, trans_ref, term_ref, gtau_ref):
    del me_ref
    regions = got_ref.shape[0]
    chunk, width = target_ref.shape
    tiles = width // LANES
    fold = regions * chunk // LANES

    for r in range(regions):
        parts = got_ref[r, tiles * chunk :].astype(F32)
        tau_ref[r] = parts[0:1] + parts[1:2] + parts[2:3]
    prefix = jnp.zeros((1, LANES), F32)
    for j in range(regions):
        r = order_ref[0, j]
        trans_ref[r] = jnp.exp(-prefix)
        prefix = prefix + tau_ref[r]
    trans_rows = stack_rows([trans_ref[r] for r in range(regions)], LANES)
    trans = trans_rows.T[:chunk]

    def tile(r, t):
        return got_ref[r, t * chunk : (t + 1) * chunk].astype(F32)

    color = [jnp.zeros((chunk, LANES), F32) for _ in range(tiles)]
    for r in range(regions):
        column = trans[:, r : r + 1]
        for t in range(tiles):
            color[t] = color[t] + column * tile(r, t)
    dcolor = []
    for t in range(tiles):
        err = color[t] - target_ref[:, t * LANES : (t + 1) * LANES].astype(F32)
        dcolor.append(err.astype(BF16))
    dcolor_f = [part.astype(F32) for part in dcolor]
    lanes = lax.broadcasted_iota(jnp.int32, (chunk, LANES), 1)
    terms = jnp.zeros((chunk, LANES), F32)
    for r in range(regions):
        q = tile(r, 0) * dcolor_f[0]
        for t in range(1, tiles):
            q = q + tile(r, t) * dcolor_f[t]
        terms = jnp.where(lanes == r, jnp.sum(q, axis=1, keepdims=True), terms)
    terms = terms * trans
    term_rows = jnp.concatenate([terms, jnp.zeros((LANES - chunk, LANES), F32)], axis=0).T
    for r in range(regions):
        term_ref[r] = term_rows[r : r + 1]
    behind = jnp.zeros((1, LANES), F32)
    for j in reversed(range(regions)):
        r = order_ref[0, j]
        gtau_ref[r] = -behind
        behind = behind + term_ref[r]
    row_lanes = lax.broadcasted_iota(jnp.int32, (fold, LANES), 1)
    extra = []
    for ref in (trans_ref, gtau_ref):
        packed = jnp.zeros((fold, LANES), F32)
        for j in range(regions // fold):
            rows = jnp.concatenate([ref[j * fold + a] for a in range(fold)], axis=0)
            rows = jnp.where(row_lanes < chunk, rows, 0.0)
            packed = packed + (pltpu.roll(rows, j * chunk, 1) if j else rows)
        extra.extend(split_parts(packed)[:2])
    for t in range(tiles):
        reply_ref[t * chunk : (t + 1) * chunk] = dcolor[t]
    reply_ref[tiles * chunk :] = jnp.concatenate(extra, axis=0).astype(BF16)


def backward_kernel(outer, flips, last, place_ref, *refs):
    pieces = sum(1 if flip else outer for flip in flips)
    chunks, refs = refs[:pieces], refs[pieces:]
    enc_ref, stat_ref, w_in_ref, w_mid_ref = refs[:4]
    if last:
        mid_before, in_before, row_before, own_ref, send_ref = refs[4:9]
    else:
        mid_out, in_out, row_out = refs[4:7]
    got_all, enc_all, hid_all, mix_all, stat_all, dpre_all, in_acc, mid_acc = refs[-8:]
    samples, regions, chunk = enc_ref.shape[:3]
    inner = regions // outer
    rays = mix_all.shape[0]
    width = w_mid_ref.shape[2]
    region_me, group_me = place_ref[0], place_ref[1]
    o_me, i_me = lax.div(region_me, inner), lax.rem(region_me, inner)

    tiles = width // LANES
    fold = regions * chunk // LANES
    length = tiles * chunk + 4 * fold
    row_ids = lax.broadcasted_iota(jnp.int32, (fold, LANES), 0)
    mine = row_ids == lax.rem(region_me, fold)
    trans_rows, gtau_rows = [], []
    lane_ids = lax.broadcasted_iota(jnp.int32, (1, LANES), 1)
    squares = row_before[1:2, :LANES] if last else jnp.zeros((1, LANES), F32)
    at, piece = 0, 0
    for flip in flips:
        for shift in range(outer):
            ref, base = (chunks[piece], shift * length) if flip else (chunks[piece + shift], 0)
            square = jnp.zeros((chunk, LANES), F32)
            for t in range(tiles):
                part = ref[base + t * chunk : base + (t + 1) * chunk]
                got_all[at : at + chunk, t * LANES : (t + 1) * LANES] = part
                square = square + part.astype(F32) * part.astype(F32)
            square = jnp.sum(jnp.sum(square, axis=0, keepdims=True), axis=1, keepdims=True)
            extra = ref[base + tiles * chunk : base + length].astype(F32)
            for rows, lo in ((trans_rows, 0), (gtau_rows, 2 * fold)):
                value = extra[lo : lo + fold] + extra[lo + fold : lo + 2 * fold]
                rows.append(jnp.sum(jnp.where(mine, value, 0.0), axis=0, keepdims=True))
            device = lax.rem(o_me + outer - shift, outer) * inner + jnp.bitwise_xor(i_me, flip)
            squares = jnp.where(lane_ids == device, square, squares)
            stat_all[at : at + chunk] = stat_ref[device]
            for k in range(samples):
                enc_all[k * rays + at : k * rays + at + chunk] = enc_ref[k, device]
            at += chunk
        piece += 1 if flip else outer
    hid_all[...] = jnp.maximum(contract(enc_all[...], w_in_ref[0], ((1,), (0,))), 0.0).astype(BF16)

    def columns(rows):
        turn = lax.rem(LANES - lax.div(region_me, fold) * chunk, LANES)
        turned = pltpu.roll(stack_rows(rows, LANES), turn, 1).T
        return jnp.concatenate([turned[:chunk, j : j + 1] for j in range(len(rows))], axis=0)

    trans_all, gtau_all = columns(trans_rows), columns(gtau_rows)
    tail_rows = stat_ref[regions]
    w_sig = jnp.concatenate([tail_rows[t : t + 1] for t in range(hid_all.shape[1] // LANES)], axis=1)
    dcolor = got_all[...]
    turned = contract(dcolor, w_mid_ref[0], ((1,), (1,)))
    block = rays
    spans = [slice(b * block, (b + 1) * block) for b in range(rays // block)]
    lanes = lax.broadcasted_iota(jnp.int32, (block, LANES), 1)
    packed = []
    for at in spans:
        pulled = trans_all[at] * turned[at]
        stat = stat_all[at]
        mix = jnp.zeros(pulled.shape, F32)
        pack = jnp.where(lanes == samples, gtau_all[at], 0.0)
        for k in range(samples):
            hidden = hid_all[k * rays + at.start : k * rays + at.stop].astype(F32)
            mix = mix + stat[:, k : k + 1] * hidden
            pack = jnp.where(lanes == k, jnp.sum(hidden * pulled, axis=1, keepdims=True), pack)
        mix_all[at] = (trans_all[at] * mix).astype(BF16)
        packed.append(pack)

    mid_part = contract(mix_all[...], dcolor, ((0,), (0,)))
    if last:
        mid_acc[...] = mid_part + mid_before[...]
    else:
        mid_out[...] = mid_part

    full = -(-rays // LANES) * LANES
    spill = [jnp.zeros((full - rays, LANES), F32)] if full > rays else []
    dots = jnp.concatenate([*packed, *spill], axis=0)
    stats = jnp.concatenate([stat_all[...], *spill], axis=0)
    tall = [slice(b * LANES, (b + 1) * LANES) for b in range(full // LANES)]
    dots = jnp.concatenate([dots[at].T[:8] for at in tall], axis=1)
    stats = jnp.concatenate([stats[at].T[: 4 * samples] for at in tall], axis=1)
    behind = -dots[samples : samples + 1]
    scales = []
    for k in reversed(range(samples)):
        remain = stats[samples + k : samples + k + 1]
        slope = stats[2 * samples + k : 2 * samples + k + 1]
        scales.insert(0, (remain * dots[k : k + 1] - behind) * slope)
        behind = behind + stats[k : k + 1] * dots[k : k + 1]
    scales = [jnp.concatenate([row[:, at] for row in scales], axis=0) for at in tall]
    scales = jnp.concatenate([stack_rows([part], LANES).T for part in scales], axis=0)

    sig = jnp.zeros((8, hid_all.shape[1]), F32)
    for at in spans:
        pulled = trans_all[at] * turned[at]
        stat, scale = stat_all[at], scales[at]
        for k in range(samples):
            rows = slice(k * rays + at.start, k * rays + at.stop)
            hidden = hid_all[rows].astype(F32)
            dz = scale[:, k : k + 1]
            dpre_all[rows] = jnp.where(hidden > 0, stat[:, k : k + 1] * pulled + dz * w_sig, 0.0).astype(BF16)
            sig = sig + jnp.sum((hidden * dz).reshape(block // 8, 8, -1), axis=0)
    sig = jnp.sum(sig, axis=0, keepdims=True)
    in_part = contract(enc_all[...], dpre_all[...], ((0,), (0,)))
    if not last:
        in_out[...] = in_part
        row_out[0:1] = sig
        row_out[1:2, :LANES] = squares
        return
    in_acc[...] = in_part + in_before[...]
    sig = sig + row_before[0:1]
    loss = jnp.sum(squares, axis=1, keepdims=True)

    groups = send_ref.shape[0] + 1
    e_rows, h_rows = in_acc.shape[0] // groups, mid_acc.shape[0] // groups
    row = lax.broadcasted_iota(jnp.int32, (PAD_ROWS, width), 0)
    tail = jnp.zeros((PAD_ROWS, width), F32)
    for j, part in enumerate(split_parts(jnp.broadcast_to(loss, (PAD_ROWS, width)))):
        tail = jnp.where(row == j + 1, part, tail)

    def fill(ref, at, group):
        ref[at, :e_rows] = in_acc[pl.ds(pl.multiple_of(group * e_rows, e_rows), e_rows), :].astype(BF16)
        ref[at, e_rows : e_rows + h_rows] = mid_acc[
            pl.ds(pl.multiple_of(group * h_rows, h_rows), h_rows), :
        ].astype(BF16)
        mine = sig[:, :h_rows]
        for other in range(1, groups):
            mine = jnp.where(group == other, sig[:, other * h_rows : (other + 1) * h_rows], mine)
        mine = jnp.concatenate([mine, jnp.zeros((1, width - h_rows), F32)], axis=1)
        ref[at, e_rows + h_rows :] = jnp.where(row == 0, mine, tail).astype(BF16)

    fill(own_ref, 0, group_me)
    for shift in range(1, groups):
        fill(send_ref, shift - 1, lax.rem(group_me + shift, groups))


def settle_kernel(scale, *refs):
    parts, (in_ref, mid_ref, sig_ref, loss_ref) = refs[:-4], refs[-4:]
    e_rows, h_rows = in_ref.shape[1], mid_ref.shape[1]

    def added(lo, hi):
        total = parts[0][0, lo:hi].astype(F32)
        for part in parts[1:]:
            total = total + part[0, lo:hi].astype(F32)
        return total

    in_ref[0] = added(0, e_rows)
    mid_ref[0] = added(e_rows, e_rows + h_rows)
    tail = added(e_rows + h_rows, e_rows + h_rows + PAD_ROWS)
    sig_ref[...] = tail[0:1, :h_rows]
    loss_ref[...] = (tail[1:2, :1] + tail[2:3, :1] + tail[3:4, :1]) * scale


def body(encoded, deltas, w_in, w_mid, w_sigma, order, target):
    _, samples, rays_dev, width_in = encoded.shape
    hidden_width, features = w_mid.shape[1:]
    regions, groups = lax.axis_size("depth"), lax.axis_size("rays")
    region_me = lax.axis_index("depth").astype(jnp.int32)
    group_me = lax.axis_index("rays").astype(jnp.int32)
    chunk = rays_dev // regions
    limit = pltpu.CompilerParams(vmem_limit_bytes=24 * MIB)
    vmem, hbm = pl.BlockSpec(memory_space=pltpu.VMEM), pl.BlockSpec(memory_space=pltpu.HBM)

    length = chunk * features // LANES + TAU_ROWS
    payload, stat = pl.pallas_call(
        forward_kernel,
        in_specs=[hbm] * 5,
        out_specs=[hbm] * 2,
        out_shape=[
            jax.ShapeDtypeStruct((regions, length, LANES), BF16),
            jax.ShapeDtypeStruct((rays_dev + chunk, LANES), F32),
        ],
        scratch_shapes=[
            pltpu.VMEM((samples, rays_dev, width_in), BF16),
            pltpu.VMEM((samples, rays_dev), F32),
            pltpu.VMEM((width_in, hidden_width), BF16),
            pltpu.VMEM((hidden_width, features), BF16),
            pltpu.VMEM((1, hidden_width), BF16),
            pltpu.VMEM((regions, length, LANES), BF16),
            pltpu.VMEM((samples, rays_dev, hidden_width), BF16),
            pltpu.VMEM((rays_dev + chunk, LANES), F32),
            pltpu.SemaphoreType.DMA((4 + samples,)),
            pltpu.SemaphoreType.DMA((1 + rays_dev // LANES,)),
        ],
        compiler_params=pltpu.CompilerParams(vmem_limit_bytes=60 * MIB),
        name="forward",
    )(encoded, deltas, w_in, w_mid, w_sigma)

    got = lax.all_to_all(payload, "depth", 0, 0)

    inner = 8
    outer = regions // inner
    fold = rays_dev // LANES
    reply_rows = features // LANES * chunk + 4 * fold
    reply = pl.pallas_call(
        composite_kernel,
        grid_spec=pltpu.PrefetchScalarGridSpec(
            num_scalar_prefetch=2,
            grid=(1,),
            in_specs=[
                pl.BlockSpec((regions, length, LANES), lambda i, order, me: (0, 0, 0)),
                pl.BlockSpec((chunk, features), lambda i, order, me: (me[0], 0)),
            ],
            out_specs=pl.BlockSpec((reply_rows, LANES), lambda i, order, me: (0, 0)),
            scratch_shapes=[pltpu.VMEM((regions, 1, LANES), F32)] * 4,
        ),
        out_shape=jax.ShapeDtypeStruct((reply_rows, LANES), BF16),
        compiler_params=limit,
        name="composite",
    )(order, region_me[None], got, target)

    def hop(value, to):
        return lax.ppermute(value, "depth", [(o * inner + i, to(o, i)) for o in range(outer) for i in range(inner)])

    across = [
        hop(reply, lambda o, i, shift=shift: (o + shift) % outer * inner + i) for shift in range(1, outer)
    ]
    bundle = jnp.concatenate([reply, *across], axis=0)
    turns = [7, 4, 3, 5, 2, 6, 1]
    onward = {}
    for flip in reversed(turns):
        onward[flip] = hop(bundle, lambda o, i, flip=flip: o * inner + (i ^ flip))

    rows = (width_in + hidden_width) // groups + PAD_ROWS
    place = jnp.stack([region_me, group_me])
    shared = (
        encoded.reshape(samples, regions, chunk, width_in),
        stat.reshape(-1, chunk, LANES),
        w_in,
        w_mid,
    )

    def backward(flips, pieces, before, out_shape):
        count = len(flips) * outer * chunk
        return pl.pallas_call(
            functools.partial(backward_kernel, outer, flips, bool(before)),
            in_specs=[pl.BlockSpec(memory_space=pltpu.SMEM)] + [vmem] * (len(pieces) + len(shared) + len(before)),
            out_specs=[vmem] * len(out_shape),
            out_shape=out_shape,
            scratch_shapes=[
                pltpu.VMEM((count, features), BF16),
                pltpu.VMEM((samples * count, width_in), BF16),
                pltpu.VMEM((samples * count, hidden_width), BF16),
                pltpu.VMEM((count, hidden_width), BF16),
                pltpu.VMEM((count, LANES), F32),
                pltpu.VMEM((samples * count, hidden_width), BF16),
                pltpu.VMEM((width_in, hidden_width), F32),
                pltpu.VMEM((hidden_width, features), F32),
            ],
            compiler_params=limit,
            cost_estimate=pl.CostEstimate(
                flops=8 * samples * count * hidden_width * (width_in + features),
                bytes_accessed=2 * samples * count * (width_in + hidden_width),
                transcendentals=0,
            ),
            name="backward_rest" if before else "backward_first",
        )(place, *pieces, *shared, *before)

    early, late = [0, *reversed(turns[:4])], [*reversed(turns[4:])]
    first = backward(
        early,
        [reply, *across, *(onward[flip] for flip in early[1:])],
        [],
        [
            jax.ShapeDtypeStruct((hidden_width, features), F32),
            jax.ShapeDtypeStruct((width_in, hidden_width), F32),
            jax.ShapeDtypeStruct((8, hidden_width), F32),
        ],
    )
    own, send = backward(
        late,
        [onward[flip] for flip in late],
        first,
        [
            jax.ShapeDtypeStruct((1, rows, features), BF16),
            jax.ShapeDtypeStruct((groups - 1, rows, features), BF16),
        ],
    )

    parts = [own]
    for shift in range(1, groups):
        ring = [(g, (g + shift) % groups) for g in range(groups)]
        parts.append(lax.ppermute(send[shift - 1 : shift], "rays", ring))

    e_rows, h_rows = width_in // groups, hidden_width // groups
    grad_in, grad_mid, grad_sigma, loss = pl.pallas_call(
        functools.partial(settle_kernel, 1.0 / (rays_dev * groups * features)),
        out_shape=[
            jax.ShapeDtypeStruct((1, e_rows, hidden_width), F32),
            jax.ShapeDtypeStruct((1, h_rows, features), F32),
            jax.ShapeDtypeStruct((1, h_rows), F32),
            jax.ShapeDtypeStruct((1, 1), F32),
        ],
        compiler_params=limit,
        name="settle",
    )(*parts)
    return (grad_in, grad_mid, grad_sigma, loss[0, 0])


def solution(mesh):
    in_specs = (
        P("depth", None, "rays", None),
        P("depth", None, "rays"),
        P("depth", None, None),
        P("depth", None, None),
        P("depth", None),
        P("rays", None),
        P("rays", None),
    )
    out_specs = (P("depth", "rays", None), P("depth", "rays", None), P("depth", "rays"), P())
    return jax.shard_map(body, mesh=mesh, in_specs=in_specs, out_specs=out_specs, check_vma=False)
```

```python
import functools

import jax
import jax.numpy as jnp
from jax import lax
from jax.experimental import pallas as pl
from jax.experimental.pallas import tpu as pltpu
from jax.sharding import PartitionSpec as P

LANES = 128
PAD_ROWS = 16
TAU_ROWS = 8
MIB = 1024 * 1024
F32 = jnp.float32
BF16 = jnp.bfloat16


def split_parts(value):
    first = value.astype(BF16).astype(F32)
    rest = value - first
    second = rest.astype(BF16).astype(F32)
    return first, second, rest - second


def stack_rows(rows, count):
    out = jnp.concatenate(rows, axis=0)
    if out.shape[0] < count:
        out = jnp.concatenate([out, jnp.zeros((count - out.shape[0], LANES), F32)], axis=0)
    return out


def contract(left, right, dims):
    return lax.dot_general(left, right, (dims, ((), ())), preferred_element_type=F32)


def forward_kernel(
    enc_hbm, delta_hbm, w_in_hbm, w_mid_hbm, w_sig_hbm, send_hbm, stat_hbm,
    enc_ref, delta_ref, w_in_ref, w_mid_ref, w_sig_ref, send_ref, hid_ref, stat_ref, sems, out_sems,
):
    samples, rays = enc_ref.shape[:2]
    blocks = rays // LANES
    chunk = rays // send_ref.shape[0]
    width = w_mid_ref.shape[1]
    copies = [
        pltpu.make_async_copy(w_in_hbm.at[0], w_in_ref, sems.at[0]),
        pltpu.make_async_copy(w_sig_hbm, w_sig_ref, sems.at[1]),
        pltpu.make_async_copy(delta_hbm.at[0], delta_ref, sems.at[2]),
        pltpu.make_async_copy(w_mid_hbm.at[0], w_mid_ref, sems.at[3]),
    ]
    enc_copies = [
        pltpu.make_async_copy(enc_hbm.at[0, k], enc_ref.at[k], sems.at[4 + k]) for k in range(samples)
    ]
    leaving = []

    def leave(source, target):
        leaving.append(pltpu.make_async_copy(source, target, out_sems.at[len(leaving)]))
        leaving[-1].start()

    for copy in [copies[0], enc_copies[0], copies[1], *enc_copies[1:], copies[2], copies[3]]:
        copy.start()
    copies[0].wait()
    copies[1].wait()
    w_in = w_in_ref[...]
    w_sig = w_sig_ref[...].astype(F32)
    lanes = lax.broadcasted_iota(jnp.int32, (rays, LANES), 1)
    pack = jnp.zeros((rays, LANES), F32)
    for k in range(samples):
        enc_copies[k].wait()
        hidden = jnp.maximum(contract(enc_ref[k], w_in, ((1,), (0,))), 0.0).astype(BF16)
        hid_ref[k] = hidden
        pack = jnp.where(lanes == k, jnp.sum(hidden.astype(F32) * w_sig, axis=1, keepdims=True), pack)

    copies[2].wait()
    copies[3].wait()
    tall = [slice(b * LANES, (b + 1) * LANES) for b in range(blocks)]
    logit = jnp.concatenate([pack[at].T[:samples] for at in tall], axis=1)
    spacing = delta_ref[...]
    small = jnp.exp(-jnp.abs(logit))
    tau = (jnp.maximum(logit, 0.0) + jnp.log1p(small)) * spacing
    slope = spacing * jnp.where(logit >= 0, 1.0, small) / (1.0 + small)
    fade = jnp.exp(-tau)
    through = jnp.ones((1, rays), F32)
    total = jnp.zeros((1, rays), F32)
    weights, remains = [], []
    for k in range(samples):
        weights.append(through * (1.0 - fade[k : k + 1]))
        through = through * fade[k : k + 1]
        remains.append(through)
        total = total + tau[k : k + 1]
    lines = jnp.concatenate(weights + remains + [slope], axis=0)
    stat = jnp.concatenate([stack_rows([lines[:, at]], LANES).T for at in tall], axis=0)
    stat_ref[:rays] = stat
    mix = stat[:, 0:1] * hid_ref[0].astype(F32)
    for k in range(1, samples):
        mix = mix + stat[:, k : k + 1] * hid_ref[k].astype(F32)
    mix = mix.astype(BF16)
    stat_ref[rays:] = stack_rows([w_sig[:, t * LANES : (t + 1) * LANES] for t in range(w_sig.shape[1] // LANES)], chunk)
    leave(stat_ref, stat_hbm)
    segment = contract(mix, w_mid_ref[...], ((1,), (0,))).astype(BF16)
    for b in range(blocks):
        tau_rows = stack_rows(list(split_parts(total[:, b * LANES : (b + 1) * LANES])), TAU_ROWS)
        for c in range(LANES // chunk):
            to = b * (LANES // chunk) + c
            for t in range(width // LANES):
                send_ref[to, t * chunk : (t + 1) * chunk] = segment[
                    to * chunk : (to + 1) * chunk, t * LANES : (t + 1) * LANES
                ]
            turned = tau_rows if c == 0 else pltpu.roll(tau_rows, LANES - c * chunk, 1)
            send_ref[to, width // LANES * chunk :] = turned.astype(BF16)
        owners = pl.ds(b * (LANES // chunk), LANES // chunk)
        leave(send_ref.at[owners], send_hbm.at[owners])
    for copy in leaving:
        copy.wait()


def composite_kernel(order_ref, me_ref, got_ref, target_ref, reply_ref, tau_ref, trans_ref, term_ref, gtau_ref):
    del me_ref
    regions = got_ref.shape[0]
    chunk, width = target_ref.shape
    tiles = width // LANES
    fold = regions * chunk // LANES

    for r in range(regions):
        parts = got_ref[r, tiles * chunk :].astype(F32)
        tau_ref[r] = parts[0:1] + parts[1:2] + parts[2:3]
    prefix = jnp.zeros((1, LANES), F32)
    for j in range(regions):
        r = order_ref[0, j]
        trans_ref[r] = jnp.exp(-prefix)
        prefix = prefix + tau_ref[r]
    trans_rows = stack_rows([trans_ref[r] for r in range(regions)], LANES)
    trans = trans_rows.T[:chunk]

    def tile(r, t):
        return got_ref[r, t * chunk : (t + 1) * chunk].astype(F32)

    color = [jnp.zeros((chunk, LANES), F32) for _ in range(tiles)]
    for r in range(regions):
        column = trans[:, r : r + 1]
        for t in range(tiles):
            color[t] = color[t] + column * tile(r, t)
    dcolor = []
    for t in range(tiles):
        err = color[t] - target_ref[:, t * LANES : (t + 1) * LANES].astype(F32)
        dcolor.append(err.astype(BF16))
    dcolor_f = [part.astype(F32) for part in dcolor]
    lanes = lax.broadcasted_iota(jnp.int32, (chunk, LANES), 1)
    terms = jnp.zeros((chunk, LANES), F32)
    for r in range(regions):
        q = tile(r, 0) * dcolor_f[0]
        for t in range(1, tiles):
            q = q + tile(r, t) * dcolor_f[t]
        terms = jnp.where(lanes == r, jnp.sum(q, axis=1, keepdims=True), terms)
    terms = terms * trans
    term_rows = jnp.concatenate([terms, jnp.zeros((LANES - chunk, LANES), F32)], axis=0).T
    for r in range(regions):
        term_ref[r] = term_rows[r : r + 1]
    behind = jnp.zeros((1, LANES), F32)
    for j in reversed(range(regions)):
        r = order_ref[0, j]
        gtau_ref[r] = -behind
        behind = behind + term_ref[r]
    row_lanes = lax.broadcasted_iota(jnp.int32, (fold, LANES), 1)
    extra = []
    for ref in (trans_ref, gtau_ref):
        packed = jnp.zeros((fold, LANES), F32)
        for j in range(regions // fold):
            rows = jnp.concatenate([ref[j * fold + a] for a in range(fold)], axis=0)
            rows = jnp.where(row_lanes < chunk, rows, 0.0)
            packed = packed + (pltpu.roll(rows, j * chunk, 1) if j else rows)
        extra.extend(split_parts(packed)[:2])
    for t in range(tiles):
        reply_ref[t * chunk : (t + 1) * chunk] = dcolor[t]
    reply_ref[tiles * chunk :] = jnp.concatenate(extra, axis=0).astype(BF16)


def backward_kernel(outer, flips, last, place_ref, *refs):
    pieces = sum(1 if flip else outer for flip in flips)
    chunks, refs = refs[:pieces], refs[pieces:]
    enc_ref, stat_ref, w_in_ref, w_mid_ref = refs[:4]
    if last:
        mid_before, in_before, row_before, own_ref, send_ref = refs[4:9]
    else:
        mid_out, in_out, row_out = refs[4:7]
    got_all, enc_all, hid_all, mix_all, stat_all, dpre_all, in_acc, mid_acc = refs[-8:]
    samples, regions, chunk = enc_ref.shape[:3]
    inner = regions // outer
    rays = mix_all.shape[0]
    width = w_mid_ref.shape[2]
    region_me, group_me = place_ref[0], place_ref[1]
    o_me, i_me = lax.div(region_me, inner), lax.rem(region_me, inner)

    tiles = width // LANES
    fold = regions * chunk // LANES
    length = tiles * chunk + 4 * fold
    row_ids = lax.broadcasted_iota(jnp.int32, (fold, LANES), 0)
    mine = row_ids == lax.rem(region_me, fold)
    trans_rows, gtau_rows = [], []
    lane_ids = lax.broadcasted_iota(jnp.int32, (1, LANES), 1)
    squares = row_before[1:2, :LANES] if last else jnp.zeros((1, LANES), F32)
    at, piece = 0, 0
    for flip in flips:
        for shift in range(outer):
            ref, base = (chunks[piece], shift * length) if flip else (chunks[piece + shift], 0)
            square = jnp.zeros((chunk, LANES), F32)
            for t in range(tiles):
                part = ref[base + t * chunk : base + (t + 1) * chunk]
                got_all[at : at + chunk, t * LANES : (t + 1) * LANES] = part
                square = square + part.astype(F32) * part.astype(F32)
            square = jnp.sum(jnp.sum(square, axis=0, keepdims=True), axis=1, keepdims=True)
            extra = ref[base + tiles * chunk : base + length].astype(F32)
            for rows, lo in ((trans_rows, 0), (gtau_rows, 2 * fold)):
                value = extra[lo : lo + fold] + extra[lo + fold : lo + 2 * fold]
                rows.append(jnp.sum(jnp.where(mine, value, 0.0), axis=0, keepdims=True))
            device = lax.rem(o_me + outer - shift, outer) * inner + jnp.bitwise_xor(i_me, flip)
            squares = jnp.where(lane_ids == device, square, squares)
            stat_all[at : at + chunk] = stat_ref[device]
            for k in range(samples):
                enc_all[k * rays + at : k * rays + at + chunk] = enc_ref[k, device]
            at += chunk
        piece += 1 if flip else outer
    hid_all[...] = jnp.maximum(contract(enc_all[...], w_in_ref[0], ((1,), (0,))), 0.0).astype(BF16)

    def columns(rows):
        turn = lax.rem(LANES - lax.div(region_me, fold) * chunk, LANES)
        turned = pltpu.roll(stack_rows(rows, LANES), turn, 1).T
        return jnp.concatenate([turned[:chunk, j : j + 1] for j in range(len(rows))], axis=0)

    trans_all, gtau_all = columns(trans_rows), columns(gtau_rows)
    tail_rows = stat_ref[regions]
    w_sig = jnp.concatenate([tail_rows[t : t + 1] for t in range(hid_all.shape[1] // LANES)], axis=1)
    dcolor = got_all[...]
    turned = contract(dcolor, w_mid_ref[0], ((1,), (1,)))
    pulled = trans_all * turned
    stat = stat_all[...]
    lanes = lax.broadcasted_iota(jnp.int32, (rays, LANES), 1)
    hidden = hid_all[...].astype(F32).reshape(samples, rays, -1)
    sums = jnp.sum(hidden * pulled[None], axis=2, keepdims=True)
    packed = jnp.where(lanes == samples, gtau_all, 0.0)
    mix = jnp.zeros(pulled.shape, F32)
    for k in range(samples):
        mix = mix + stat[:, k : k + 1] * hidden[k]
        packed = jnp.where(lanes == k, sums[k], packed)
    mix_all[...] = (trans_all * mix).astype(BF16)

    mid_part = contract(mix_all[...], dcolor, ((0,), (0,)))
    if last:
        mid_acc[...] = mid_part + mid_before[...]
    else:
        mid_out[...] = mid_part

    full = -(-rays // LANES) * LANES
    spill = [jnp.zeros((full - rays, LANES), F32)] if full > rays else []
    dots = jnp.concatenate([packed, *spill], axis=0)
    stats = jnp.concatenate([stat, *spill], axis=0)
    tall = [slice(b * LANES, (b + 1) * LANES) for b in range(full // LANES)]
    dots = jnp.concatenate([dots[at].T[:8] for at in tall], axis=1)
    stats = jnp.concatenate([stats[at].T[: 4 * samples] for at in tall], axis=1)
    behind = -dots[samples : samples + 1]
    scales = []
    for k in reversed(range(samples)):
        remain = stats[samples + k : samples + k + 1]
        slope = stats[2 * samples + k : 2 * samples + k + 1]
        scales.insert(0, (remain * dots[k : k + 1] - behind) * slope)
        behind = behind + stats[k : k + 1] * dots[k : k + 1]
    scales = [jnp.concatenate([row[:, at] for row in scales], axis=0) for at in tall]
    scales = jnp.concatenate([stack_rows([part], LANES).T for part in scales], axis=0)

    sig = jnp.zeros((8, hid_all.shape[1]), F32)
    for k in range(samples):
        rows = slice(k * rays, (k + 1) * rays)
        hidden = hid_all[rows].astype(F32)
        dz = scales[:rays, k : k + 1]
        dpre_all[rows] = jnp.where(hidden > 0, stat[:, k : k + 1] * pulled + dz * w_sig, 0.0).astype(BF16)
        sig = sig + jnp.sum((hidden * dz).reshape(rays // 8, 8, -1), axis=0)
    sig = jnp.sum(sig, axis=0, keepdims=True)
    in_part = contract(enc_all[...], dpre_all[...], ((0,), (0,)))
    if not last:
        in_out[...] = in_part
        row_out[0:1] = sig
        row_out[1:2, :LANES] = squares
        return
    in_acc[...] = in_part + in_before[...]
    sig = sig + row_before[0:1]
    loss = jnp.sum(squares, axis=1, keepdims=True)

    groups = send_ref.shape[0] + 1
    e_rows, h_rows = in_acc.shape[0] // groups, mid_acc.shape[0] // groups
    row = lax.broadcasted_iota(jnp.int32, (PAD_ROWS, width), 0)
    tail = jnp.zeros((PAD_ROWS, width), F32)
    for j, part in enumerate(split_parts(jnp.broadcast_to(loss, (PAD_ROWS, width)))):
        tail = jnp.where(row == j + 1, part, tail)

    def fill(ref, at, group):
        ref[at, :e_rows] = in_acc[pl.ds(pl.multiple_of(group * e_rows, e_rows), e_rows), :].astype(BF16)
        ref[at, e_rows : e_rows + h_rows] = mid_acc[
            pl.ds(pl.multiple_of(group * h_rows, h_rows), h_rows), :
        ].astype(BF16)
        mine = sig[:, :h_rows]
        for other in range(1, groups):
            mine = jnp.where(group == other, sig[:, other * h_rows : (other + 1) * h_rows], mine)
        mine = jnp.concatenate([mine, jnp.zeros((1, width - h_rows), F32)], axis=1)
        ref[at, e_rows + h_rows :] = jnp.where(row == 0, mine, tail).astype(BF16)

    fill(own_ref, 0, group_me)
    for shift in range(1, groups):
        fill(send_ref, shift - 1, lax.rem(group_me + shift, groups))


def settle_kernel(scale, *refs):
    parts, (in_ref, mid_ref, sig_ref, loss_ref) = refs[:-4], refs[-4:]
    e_rows, h_rows = in_ref.shape[1], mid_ref.shape[1]

    def added(lo, hi):
        total = parts[0][0, lo:hi].astype(F32)
        for part in parts[1:]:
            total = total + part[0, lo:hi].astype(F32)
        return total

    in_ref[0] = added(0, e_rows)
    mid_ref[0] = added(e_rows, e_rows + h_rows)
    tail = added(e_rows + h_rows, e_rows + h_rows + PAD_ROWS)
    sig_ref[...] = tail[0:1, :h_rows]
    loss_ref[...] = (tail[1:2, :1] + tail[2:3, :1] + tail[3:4, :1]) * scale


def body(encoded, deltas, w_in, w_mid, w_sigma, order, target):
    _, samples, rays_dev, width_in = encoded.shape
    hidden_width, features = w_mid.shape[1:]
    regions, groups = lax.axis_size("depth"), lax.axis_size("rays")
    region_me = lax.axis_index("depth").astype(jnp.int32)
    group_me = lax.axis_index("rays").astype(jnp.int32)
    chunk = rays_dev // regions
    limit = pltpu.CompilerParams(vmem_limit_bytes=24 * MIB)
    vmem, hbm = pl.BlockSpec(memory_space=pltpu.VMEM), pl.BlockSpec(memory_space=pltpu.HBM)

    length = chunk * features // LANES + TAU_ROWS
    payload, stat = pl.pallas_call(
        forward_kernel,
        in_specs=[hbm] * 5,
        out_specs=[hbm] * 2,
        out_shape=[
            jax.ShapeDtypeStruct((regions, length, LANES), BF16),
            jax.ShapeDtypeStruct((rays_dev + chunk, LANES), F32),
        ],
        scratch_shapes=[
            pltpu.VMEM((samples, rays_dev, width_in), BF16),
            pltpu.VMEM((samples, rays_dev), F32),
            pltpu.VMEM((width_in, hidden_width), BF16),
            pltpu.VMEM((hidden_width, features), BF16),
            pltpu.VMEM((1, hidden_width), BF16),
            pltpu.VMEM((regions, length, LANES), BF16),
            pltpu.VMEM((samples, rays_dev, hidden_width), BF16),
            pltpu.VMEM((rays_dev + chunk, LANES), F32),
            pltpu.SemaphoreType.DMA((4 + samples,)),
            pltpu.SemaphoreType.DMA((1 + rays_dev // LANES,)),
        ],
        compiler_params=pltpu.CompilerParams(vmem_limit_bytes=60 * MIB),
        name="forward",
    )(encoded, deltas, w_in, w_mid, w_sigma)

    got = lax.all_to_all(payload, "depth", 0, 0)

    inner = 8
    outer = regions // inner
    fold = rays_dev // LANES
    reply_rows = features // LANES * chunk + 4 * fold
    reply = pl.pallas_call(
        composite_kernel,
        grid_spec=pltpu.PrefetchScalarGridSpec(
            num_scalar_prefetch=2,
            grid=(1,),
            in_specs=[
                pl.BlockSpec((regions, length, LANES), lambda i, order, me: (0, 0, 0)),
                pl.BlockSpec((chunk, features), lambda i, order, me: (me[0], 0)),
            ],
            out_specs=pl.BlockSpec((reply_rows, LANES), lambda i, order, me: (0, 0)),
            scratch_shapes=[pltpu.VMEM((regions, 1, LANES), F32)] * 4,
        ),
        out_shape=jax.ShapeDtypeStruct((reply_rows, LANES), BF16),
        compiler_params=limit,
        name="composite",
    )(order, region_me[None], got, target)

    def hop(value, to):
        return lax.ppermute(value, "depth", [(o * inner + i, to(o, i)) for o in range(outer) for i in range(inner)])

    across = [
        hop(reply, lambda o, i, shift=shift: (o + shift) % outer * inner + i) for shift in range(1, outer)
    ]
    bundle = jnp.concatenate([reply, *across], axis=0)
    turns = [7, 4, 3, 5, 2, 6, 1]
    onward = {}
    for flip in reversed(turns):
        onward[flip] = hop(bundle, lambda o, i, flip=flip: o * inner + (i ^ flip))

    rows = (width_in + hidden_width) // groups + PAD_ROWS
    place = jnp.stack([region_me, group_me])
    shared = (
        encoded.reshape(samples, regions, chunk, width_in),
        stat.reshape(-1, chunk, LANES),
        w_in,
        w_mid,
    )

    def backward(flips, pieces, before, out_shape):
        count = len(flips) * outer * chunk
        return pl.pallas_call(
            functools.partial(backward_kernel, outer, flips, bool(before)),
            in_specs=[pl.BlockSpec(memory_space=pltpu.SMEM)] + [vmem] * (len(pieces) + len(shared) + len(before)),
            out_specs=[vmem] * len(out_shape),
            out_shape=out_shape,
            scratch_shapes=[
                pltpu.VMEM((count, features), BF16),
                pltpu.VMEM((samples * count, width_in), BF16),
                pltpu.VMEM((samples * count, hidden_width), BF16),
                pltpu.VMEM((count, hidden_width), BF16),
                pltpu.VMEM((count, LANES), F32),
                pltpu.VMEM((samples * count, hidden_width), BF16),
                pltpu.VMEM((width_in, hidden_width), F32),
                pltpu.VMEM((hidden_width, features), F32),
            ],
            compiler_params=limit,
            cost_estimate=pl.CostEstimate(
                flops=8 * samples * count * hidden_width * (width_in + features),
                bytes_accessed=2 * samples * count * (width_in + hidden_width),
                transcendentals=0,
            ),
            name="backward_rest" if before else "backward_first",
        )(place, *pieces, *shared, *before)

    early, late = [0, *reversed(turns[:4])], [*reversed(turns[4:])]
    first = backward(
        early,
        [reply, *across, *(onward[flip] for flip in early[1:])],
        [],
        [
            jax.ShapeDtypeStruct((hidden_width, features), F32),
            jax.ShapeDtypeStruct((width_in, hidden_width), F32),
            jax.ShapeDtypeStruct((8, hidden_width), F32),
        ],
    )
    own, send = backward(
        late,
        [onward[flip] for flip in late],
        first,
        [
            jax.ShapeDtypeStruct((1, rows, features), BF16),
            jax.ShapeDtypeStruct((groups - 1, rows, features), BF16),
        ],
    )

    parts = [own]
    for shift in range(1, groups):
        ring = [(g, (g + shift) % groups) for g in range(groups)]
        parts.append(lax.ppermute(send[shift - 1 : shift], "rays", ring))

    e_rows, h_rows = width_in // groups, hidden_width // groups
    grad_in, grad_mid, grad_sigma, loss = pl.pallas_call(
        functools.partial(settle_kernel, 1.0 / (rays_dev * groups * features)),
        out_shape=[
            jax.ShapeDtypeStruct((1, e_rows, hidden_width), F32),
            jax.ShapeDtypeStruct((1, h_rows, features), F32),
            jax.ShapeDtypeStruct((1, h_rows), F32),
            jax.ShapeDtypeStruct((1, 1), F32),
        ],
        compiler_params=limit,
        name="settle",
    )(*parts)
    return (grad_in, grad_mid, grad_sigma, loss[0, 0])


def solution(mesh):
    in_specs = (
        P("depth", None, "rays", None),
        P("depth", None, "rays"),
        P("depth", None, None),
        P("depth", None, None),
        P("depth", None),
        P("rays", None),
        P("rays", None),
    )
    out_specs = (P("depth", "rays", None), P("depth", "rays", None), P("depth", "rays"), P())
    return jax.shard_map(body, mesh=mesh, in_specs=in_specs, out_specs=out_specs, check_vma=False)
```

```python
import functools

import jax
import jax.numpy as jnp
from jax import lax
from jax.experimental import pallas as pl
from jax.experimental.pallas import tpu as pltpu
from jax.sharding import PartitionSpec as P

LANES = 128
PAD_ROWS = 16
TAU_ROWS = 8
MIB = 1024 * 1024
F32 = jnp.float32
BF16 = jnp.bfloat16


def split_parts(value):
    first = value.astype(BF16).astype(F32)
    rest = value - first
    second = rest.astype(BF16).astype(F32)
    return first, second, rest - second


def stack_rows(rows, count):
    out = jnp.concatenate(rows, axis=0)
    if out.shape[0] < count:
        out = jnp.concatenate([out, jnp.zeros((count - out.shape[0], LANES), F32)], axis=0)
    return out


def contract(left, right, dims):
    return lax.dot_general(left, right, (dims, ((), ())), preferred_element_type=F32)


def forward_kernel(
    enc_hbm, delta_hbm, w_in_hbm, w_mid_hbm, w_sig_hbm, send_hbm, stat_hbm,
    enc_ref, delta_ref, w_in_ref, w_mid_ref, w_sig_ref, send_ref, hid_ref, stat_ref, sems, out_sems,
):
    samples, rays = enc_ref.shape[:2]
    blocks = rays // LANES
    chunk = rays // send_ref.shape[0]
    width = w_mid_ref.shape[1]
    copies = [
        pltpu.make_async_copy(w_in_hbm.at[0], w_in_ref, sems.at[0]),
        pltpu.make_async_copy(w_sig_hbm, w_sig_ref, sems.at[1]),
        pltpu.make_async_copy(delta_hbm.at[0], delta_ref, sems.at[2]),
        pltpu.make_async_copy(w_mid_hbm.at[0], w_mid_ref, sems.at[3]),
    ]
    enc_copies = [
        pltpu.make_async_copy(enc_hbm.at[0, k], enc_ref.at[k], sems.at[4 + k]) for k in range(samples)
    ]
    leaving = []

    def leave(source, target):
        leaving.append(pltpu.make_async_copy(source, target, out_sems.at[len(leaving)]))
        leaving[-1].start()

    for copy in [copies[0], enc_copies[0], copies[1], *enc_copies[1:], copies[2], copies[3]]:
        copy.start()
    copies[0].wait()
    copies[1].wait()
    w_in = w_in_ref[...]
    w_sig = w_sig_ref[...].astype(F32)
    lanes = lax.broadcasted_iota(jnp.int32, (rays, LANES), 1)
    pack = jnp.zeros((rays, LANES), F32)
    for k in range(samples):
        enc_copies[k].wait()
        hidden = jnp.maximum(contract(enc_ref[k], w_in, ((1,), (0,))), 0.0).astype(BF16)
        hid_ref[k] = hidden
        pack = jnp.where(lanes == k, jnp.sum(hidden.astype(F32) * w_sig, axis=1, keepdims=True), pack)

    copies[2].wait()
    copies[3].wait()
    tall = [slice(b * LANES, (b + 1) * LANES) for b in range(blocks)]
    logit = jnp.concatenate([pack[at].T[:samples] for at in tall], axis=1)
    spacing = delta_ref[...]
    small = jnp.exp(-jnp.abs(logit))
    tau = (jnp.maximum(logit, 0.0) + jnp.log1p(small)) * spacing
    slope = spacing * jnp.where(logit >= 0, 1.0, small) / (1.0 + small)
    fade = jnp.exp(-tau)
    through = jnp.ones((1, rays), F32)
    total = jnp.zeros((1, rays), F32)
    weights, remains = [], []
    for k in range(samples):
        weights.append(through * (1.0 - fade[k : k + 1]))
        through = through * fade[k : k + 1]
        remains.append(through)
        total = total + tau[k : k + 1]
    lines = jnp.concatenate(weights + remains + [slope], axis=0)
    stat = jnp.concatenate([stack_rows([lines[:, at]], LANES).T for at in tall], axis=0)
    stat_ref[:rays] = stat
    mix = stat[:, 0:1] * hid_ref[0].astype(F32)
    for k in range(1, samples):
        mix = mix + stat[:, k : k + 1] * hid_ref[k].astype(F32)
    mix = mix.astype(BF16)
    stat_ref[rays:] = stack_rows([w_sig[:, t * LANES : (t + 1) * LANES] for t in range(w_sig.shape[1] // LANES)], chunk)
    leave(stat_ref, stat_hbm)
    segment = contract(mix, w_mid_ref[...], ((1,), (0,))).astype(BF16)
    for b in range(blocks):
        tau_rows = stack_rows(list(split_parts(total[:, b * LANES : (b + 1) * LANES])), TAU_ROWS)
        for c in range(LANES // chunk):
            to = b * (LANES // chunk) + c
            for t in range(width // LANES):
                send_ref[to, t * chunk : (t + 1) * chunk] = segment[
                    to * chunk : (to + 1) * chunk, t * LANES : (t + 1) * LANES
                ]
            turned = tau_rows if c == 0 else pltpu.roll(tau_rows, LANES - c * chunk, 1)
            send_ref[to, width // LANES * chunk :] = turned.astype(BF16)
        owners = pl.ds(b * (LANES // chunk), LANES // chunk)
        leave(send_ref.at[owners], send_hbm.at[owners])
    for copy in leaving:
        copy.wait()


def composite_kernel(order_ref, me_ref, got_ref, target_ref, reply_ref, tau_ref, trans_ref, term_ref, gtau_ref):
    del me_ref
    regions = got_ref.shape[0]
    chunk, width = target_ref.shape
    tiles = width // LANES
    fold = regions * chunk // LANES

    for r in range(regions):
        parts = got_ref[r, tiles * chunk :].astype(F32)
        tau_ref[r] = parts[0:1] + parts[1:2] + parts[2:3]
    prefix = jnp.zeros((1, LANES), F32)
    for j in range(regions):
        r = order_ref[0, j]
        trans_ref[r] = jnp.exp(-prefix)
        prefix = prefix + tau_ref[r]
    trans_rows = stack_rows([trans_ref[r] for r in range(regions)], LANES)
    trans = trans_rows.T[:chunk]

    def tile(t):
        return got_ref[:, t * chunk : (t + 1) * chunk].astype(F32)

    columns = jnp.stack([trans[:, r : r + 1] for r in range(regions)], axis=0)
    color = [jnp.sum(columns * tile(t), axis=0) for t in range(tiles)]
    dcolor = []
    for t in range(tiles):
        err = color[t] - target_ref[:, t * LANES : (t + 1) * LANES].astype(F32)
        dcolor.append(err.astype(BF16))
    dcolor_f = [part.astype(F32) for part in dcolor]
    lanes = lax.broadcasted_iota(jnp.int32, (chunk, LANES), 1)
    terms = jnp.zeros((chunk, LANES), F32)
    q = tile(0) * dcolor_f[0][None]
    for t in range(1, tiles):
        q = q + tile(t) * dcolor_f[t][None]
    q = jnp.sum(q, axis=2, keepdims=True)
    for r in range(regions):
        terms = jnp.where(lanes == r, q[r], terms)
    terms = terms * trans
    term_rows = jnp.concatenate([terms, jnp.zeros((LANES - chunk, LANES), F32)], axis=0).T
    for r in range(regions):
        term_ref[r] = term_rows[r : r + 1]
    behind = jnp.zeros((1, LANES), F32)
    for j in reversed(range(regions)):
        r = order_ref[0, j]
        gtau_ref[r] = -behind
        behind = behind + term_ref[r]
    row_lanes = lax.broadcasted_iota(jnp.int32, (fold, LANES), 1)
    extra = []
    for ref in (trans_ref, gtau_ref):
        packed = jnp.zeros((fold, LANES), F32)
        for j in range(regions // fold):
            rows = jnp.concatenate([ref[j * fold + a] for a in range(fold)], axis=0)
            rows = jnp.where(row_lanes < chunk, rows, 0.0)
            packed = packed + (pltpu.roll(rows, j * chunk, 1) if j else rows)
        extra.extend(split_parts(packed)[:2])
    for t in range(tiles):
        reply_ref[t * chunk : (t + 1) * chunk] = dcolor[t]
    reply_ref[tiles * chunk :] = jnp.concatenate(extra, axis=0).astype(BF16)


def backward_kernel(outer, flips, last, place_ref, *refs):
    pieces = sum(1 if flip else outer for flip in flips)
    chunks, refs = refs[:pieces], refs[pieces:]
    enc_ref, stat_ref, w_in_ref, w_mid_ref = refs[:4]
    if last:
        mid_before, in_before, row_before, own_ref, send_ref = refs[4:9]
    else:
        mid_out, in_out, row_out = refs[4:7]
    got_all, enc_all, hid_all, mix_all, stat_all, dpre_all, in_acc, mid_acc = refs[-8:]
    samples, regions, chunk = enc_ref.shape[:3]
    inner = regions // outer
    rays = mix_all.shape[0]
    width = w_mid_ref.shape[2]
    region_me, group_me = place_ref[0], place_ref[1]
    o_me, i_me = lax.div(region_me, inner), lax.rem(region_me, inner)

    tiles = width // LANES
    fold = regions * chunk // LANES
    length = tiles * chunk + 4 * fold
    row_ids = lax.broadcasted_iota(jnp.int32, (fold, LANES), 0)
    mine = row_ids == lax.rem(region_me, fold)
    trans_rows, gtau_rows = [], []
    lane_ids = lax.broadcasted_iota(jnp.int32, (1, LANES), 1)
    squares = row_before[1:2, :LANES] if last else jnp.zeros((1, LANES), F32)
    at, piece = 0, 0
    for flip in flips:
        for shift in range(outer):
            ref, base = (chunks[piece], shift * length) if flip else (chunks[piece + shift], 0)
            square = jnp.zeros((chunk, LANES), F32)
            for t in range(tiles):
                part = ref[base + t * chunk : base + (t + 1) * chunk]
                got_all[at : at + chunk, t * LANES : (t + 1) * LANES] = part
                square = square + part.astype(F32) * part.astype(F32)
            square = jnp.sum(jnp.sum(square, axis=0, keepdims=True), axis=1, keepdims=True)
            extra = ref[base + tiles * chunk : base + length].astype(F32)
            for rows, lo in ((trans_rows, 0), (gtau_rows, 2 * fold)):
                value = extra[lo : lo + fold] + extra[lo + fold : lo + 2 * fold]
                rows.append(jnp.sum(jnp.where(mine, value, 0.0), axis=0, keepdims=True))
            device = lax.rem(o_me + outer - shift, outer) * inner + jnp.bitwise_xor(i_me, flip)
            squares = jnp.where(lane_ids == device, square, squares)
            stat_all[at : at + chunk] = stat_ref[device]
            for k in range(samples):
                enc_all[k * rays + at : k * rays + at + chunk] = enc_ref[k, device]
            at += chunk
        piece += 1 if flip else outer
    hid_all[...] = jnp.maximum(contract(enc_all[...], w_in_ref[0], ((1,), (0,))), 0.0).astype(BF16)

    def columns(rows):
        turn = lax.rem(LANES - lax.div(region_me, fold) * chunk, LANES)
        turned = pltpu.roll(stack_rows(rows, LANES), turn, 1).T
        return jnp.concatenate([turned[:chunk, j : j + 1] for j in range(len(rows))], axis=0)

    trans_all, gtau_all = columns(trans_rows), columns(gtau_rows)
    tail_rows = stat_ref[regions]
    w_sig = jnp.concatenate([tail_rows[t : t + 1] for t in range(hid_all.shape[1] // LANES)], axis=1)
    dcolor = got_all[...]
    turned = contract(dcolor, w_mid_ref[0], ((1,), (1,)))
    pulled = trans_all * turned
    stat = stat_all[...]
    lanes = lax.broadcasted_iota(jnp.int32, (rays, LANES), 1)
    hidden = hid_all[...].astype(F32).reshape(samples, rays, -1)
    sums = jnp.sum(hidden * pulled[None], axis=2, keepdims=True)
    packed = jnp.where(lanes == samples, gtau_all, 0.0)
    mix = jnp.zeros(pulled.shape, F32)
    for k in range(samples):
        mix = mix + stat[:, k : k + 1] * hidden[k]
        packed = jnp.where(lanes == k, sums[k], packed)
    mix_all[...] = (trans_all * mix).astype(BF16)

    mid_part = contract(mix_all[...], dcolor, ((0,), (0,)))
    if last:
        mid_acc[...] = mid_part + mid_before[...]
    else:
        mid_out[...] = mid_part

    full = -(-rays // LANES) * LANES
    spill = [jnp.zeros((full - rays, LANES), F32)] if full > rays else []
    dots = jnp.concatenate([packed, *spill], axis=0)
    stats = jnp.concatenate([stat, *spill], axis=0)
    tall = [slice(b * LANES, (b + 1) * LANES) for b in range(full // LANES)]
    dots = jnp.concatenate([dots[at].T[:8] for at in tall], axis=1)
    stats = jnp.concatenate([stats[at].T[: 4 * samples] for at in tall], axis=1)
    behind = -dots[samples : samples + 1]
    scales = []
    for k in reversed(range(samples)):
        remain = stats[samples + k : samples + k + 1]
        slope = stats[2 * samples + k : 2 * samples + k + 1]
        scales.insert(0, (remain * dots[k : k + 1] - behind) * slope)
        behind = behind + stats[k : k + 1] * dots[k : k + 1]
    scales = [jnp.concatenate([row[:, at] for row in scales], axis=0) for at in tall]
    scales = jnp.concatenate([stack_rows([part], LANES).T for part in scales], axis=0)

    sig = jnp.zeros((8, hid_all.shape[1]), F32)
    for k in range(samples):
        rows = slice(k * rays, (k + 1) * rays)
        hidden = hid_all[rows].astype(F32)
        dz = scales[:rays, k : k + 1]
        dpre_all[rows] = jnp.where(hidden > 0, stat[:, k : k + 1] * pulled + dz * w_sig, 0.0).astype(BF16)
        sig = sig + jnp.sum((hidden * dz).reshape(rays // 8, 8, -1), axis=0)
    sig = jnp.sum(sig, axis=0, keepdims=True)
    in_part = contract(enc_all[...], dpre_all[...], ((0,), (0,)))
    if not last:
        in_out[...] = in_part
        row_out[0:1] = sig
        row_out[1:2, :LANES] = squares
        return
    in_acc[...] = in_part + in_before[...]
    sig = sig + row_before[0:1]
    loss = jnp.sum(squares, axis=1, keepdims=True)

    groups = send_ref.shape[0] + 1
    e_rows, h_rows = in_acc.shape[0] // groups, mid_acc.shape[0] // groups
    row = lax.broadcasted_iota(jnp.int32, (PAD_ROWS, width), 0)
    tail = jnp.zeros((PAD_ROWS, width), F32)
    for j, part in enumerate(split_parts(jnp.broadcast_to(loss, (PAD_ROWS, width)))):
        tail = jnp.where(row == j + 1, part, tail)

    def fill(ref, at, group):
        ref[at, :e_rows] = in_acc[pl.ds(pl.multiple_of(group * e_rows, e_rows), e_rows), :].astype(BF16)
        ref[at, e_rows : e_rows + h_rows] = mid_acc[
            pl.ds(pl.multiple_of(group * h_rows, h_rows), h_rows), :
        ].astype(BF16)
        mine = sig[:, :h_rows]
        for other in range(1, groups):
            mine = jnp.where(group == other, sig[:, other * h_rows : (other + 1) * h_rows], mine)
        mine = jnp.concatenate([mine, jnp.zeros((1, width - h_rows), F32)], axis=1)
        ref[at, e_rows + h_rows :] = jnp.where(row == 0, mine, tail).astype(BF16)

    fill(own_ref, 0, group_me)
    for shift in range(1, groups):
        fill(send_ref, shift - 1, lax.rem(group_me + shift, groups))


def settle_kernel(scale, *refs):
    parts, (in_ref, mid_ref, sig_ref, loss_ref) = refs[:-4], refs[-4:]
    e_rows, h_rows = in_ref.shape[1], mid_ref.shape[1]

    def added(lo, hi):
        total = parts[0][0, lo:hi].astype(F32)
        for part in parts[1:]:
            total = total + part[0, lo:hi].astype(F32)
        return total

    in_ref[0] = added(0, e_rows)
    mid_ref[0] = added(e_rows, e_rows + h_rows)
    tail = added(e_rows + h_rows, e_rows + h_rows + PAD_ROWS)
    sig_ref[...] = tail[0:1, :h_rows]
    loss_ref[...] = (tail[1:2, :1] + tail[2:3, :1] + tail[3:4, :1]) * scale


def body(encoded, deltas, w_in, w_mid, w_sigma, order, target):
    _, samples, rays_dev, width_in = encoded.shape
    hidden_width, features = w_mid.shape[1:]
    regions, groups = lax.axis_size("depth"), lax.axis_size("rays")
    region_me = lax.axis_index("depth").astype(jnp.int32)
    group_me = lax.axis_index("rays").astype(jnp.int32)
    chunk = rays_dev // regions
    limit = pltpu.CompilerParams(vmem_limit_bytes=24 * MIB)
    vmem, hbm = pl.BlockSpec(memory_space=pltpu.VMEM), pl.BlockSpec(memory_space=pltpu.HBM)

    length = chunk * features // LANES + TAU_ROWS
    payload, stat = pl.pallas_call(
        forward_kernel,
        in_specs=[hbm] * 5,
        out_specs=[hbm] * 2,
        out_shape=[
            jax.ShapeDtypeStruct((regions, length, LANES), BF16),
            jax.ShapeDtypeStruct((rays_dev + chunk, LANES), F32),
        ],
        scratch_shapes=[
            pltpu.VMEM((samples, rays_dev, width_in), BF16),
            pltpu.VMEM((samples, rays_dev), F32),
            pltpu.VMEM((width_in, hidden_width), BF16),
            pltpu.VMEM((hidden_width, features), BF16),
            pltpu.VMEM((1, hidden_width), BF16),
            pltpu.VMEM((regions, length, LANES), BF16),
            pltpu.VMEM((samples, rays_dev, hidden_width), BF16),
            pltpu.VMEM((rays_dev + chunk, LANES), F32),
            pltpu.SemaphoreType.DMA((4 + samples,)),
            pltpu.SemaphoreType.DMA((1 + rays_dev // LANES,)),
        ],
        compiler_params=pltpu.CompilerParams(vmem_limit_bytes=60 * MIB),
        name="forward",
    )(encoded, deltas, w_in, w_mid, w_sigma)

    got = lax.all_to_all(payload, "depth", 0, 0)

    inner = 8
    outer = regions // inner
    fold = rays_dev // LANES
    reply_rows = features // LANES * chunk + 4 * fold
    reply = pl.pallas_call(
        composite_kernel,
        grid_spec=pltpu.PrefetchScalarGridSpec(
            num_scalar_prefetch=2,
            grid=(1,),
            in_specs=[
                pl.BlockSpec((regions, length, LANES), lambda i, order, me: (0, 0, 0)),
                pl.BlockSpec((chunk, features), lambda i, order, me: (me[0], 0)),
            ],
            out_specs=pl.BlockSpec((reply_rows, LANES), lambda i, order, me: (0, 0)),
            scratch_shapes=[pltpu.VMEM((regions, 1, LANES), F32)] * 4,
        ),
        out_shape=jax.ShapeDtypeStruct((reply_rows, LANES), BF16),
        compiler_params=limit,
        name="composite",
    )(order, region_me[None], got, target)

    def hop(value, to):
        return lax.ppermute(value, "depth", [(o * inner + i, to(o, i)) for o in range(outer) for i in range(inner)])

    across = [
        hop(reply, lambda o, i, shift=shift: (o + shift) % outer * inner + i) for shift in range(1, outer)
    ]
    bundle = jnp.concatenate([reply, *across], axis=0)
    turns = [7, 4, 3, 5, 2, 6, 1]
    onward = {}
    for flip in reversed(turns):
        onward[flip] = hop(bundle, lambda o, i, flip=flip: o * inner + (i ^ flip))

    rows = (width_in + hidden_width) // groups + PAD_ROWS
    place = jnp.stack([region_me, group_me])
    shared = (
        encoded.reshape(samples, regions, chunk, width_in),
        stat.reshape(-1, chunk, LANES),
        w_in,
        w_mid,
    )

    def backward(flips, pieces, before, out_shape):
        count = len(flips) * outer * chunk
        return pl.pallas_call(
            functools.partial(backward_kernel, outer, flips, bool(before)),
            in_specs=[pl.BlockSpec(memory_space=pltpu.SMEM)] + [vmem] * (len(pieces) + len(shared) + len(before)),
            out_specs=[vmem] * len(out_shape),
            out_shape=out_shape,
            scratch_shapes=[
                pltpu.VMEM((count, features), BF16),
                pltpu.VMEM((samples * count, width_in), BF16),
                pltpu.VMEM((samples * count, hidden_width), BF16),
                pltpu.VMEM((count, hidden_width), BF16),
                pltpu.VMEM((count, LANES), F32),
                pltpu.VMEM((samples * count, hidden_width), BF16),
                pltpu.VMEM((width_in, hidden_width), F32),
                pltpu.VMEM((hidden_width, features), F32),
            ],
            compiler_params=limit,
            cost_estimate=pl.CostEstimate(
                flops=8 * samples * count * hidden_width * (width_in + features),
                bytes_accessed=2 * samples * count * (width_in + hidden_width),
                transcendentals=0,
            ),
            name="backward_rest" if before else "backward_first",
        )(place, *pieces, *shared, *before)

    early, late = [0, *reversed(turns[:4])], [*reversed(turns[4:])]
    first = backward(
        early,
        [reply, *across, *(onward[flip] for flip in early[1:])],
        [],
        [
            jax.ShapeDtypeStruct((hidden_width, features), F32),
            jax.ShapeDtypeStruct((width_in, hidden_width), F32),
            jax.ShapeDtypeStruct((8, hidden_width), F32),
        ],
    )
    own, send = backward(
        late,
        [onward[flip] for flip in late],
        first,
        [
            jax.ShapeDtypeStruct((1, rows, features), BF16),
            jax.ShapeDtypeStruct((groups - 1, rows, features), BF16),
        ],
    )

    parts = [own]
    for shift in range(1, groups):
        ring = [(g, (g + shift) % groups) for g in range(groups)]
        parts.append(lax.ppermute(send[shift - 1 : shift], "rays", ring))

    e_rows, h_rows = width_in // groups, hidden_width // groups
    grad_in, grad_mid, grad_sigma, loss = pl.pallas_call(
        functools.partial(settle_kernel, 1.0 / (rays_dev * groups * features)),
        out_shape=[
            jax.ShapeDtypeStruct((1, e_rows, hidden_width), F32),
            jax.ShapeDtypeStruct((1, h_rows, features), F32),
            jax.ShapeDtypeStruct((1, h_rows), F32),
            jax.ShapeDtypeStruct((1, 1), F32),
        ],
        compiler_params=limit,
        name="settle",
    )(*parts)
    return (grad_in, grad_mid, grad_sigma, loss[0, 0])


def solution(mesh):
    in_specs = (
        P("depth", None, "rays", None),
        P("depth", None, "rays"),
        P("depth", None, None),
        P("depth", None, None),
        P("depth", None),
        P("rays", None),
        P("rays", None),
    )
    out_specs = (P("depth", "rays", None), P("depth", "rays", None), P("depth", "rays"), P())
    return jax.shard_map(body, mesh=mesh, in_specs=in_specs, out_specs=out_specs, check_vma=False)
```
